128 devices in a mesh: crop: 4 (over z), scene: 32 (over x, y, core).
Axes of the slice: x: 4, y: 4, z: 4, core: 2. Of those that a mesh axis runs over, the one named last changes fastest.
Arguments:
- fine_feats: bfloat16 [4, 196608, 128], P('crop', 'scene'), may hold values from -6 to 6
- out_grad: bfloat16 [4, 196608, 128], P('crop', 'scene'), may hold values from -6 to 6
- pre_act: bfloat16 [4, 32, 32, 2, 64, 256], P('crop', 'scene'), may hold values from -6 to 6
- deep_grad: bfloat16 [4, 32, 32, 2, 64, 256], P('crop', 'scene'), may hold values from -6 to 6
- down_weight: bfloat16 [8, 128, 256], replicated, may hold values from -0.3125 to 0.3125
- up_weight: bfloat16 [8, 256, 128], replicated, may hold values from -0.375 to 0.375
- block_owner: int32 [4, 1024, 1], P('crop', 'scene'), may hold values from 0 to 31; in each aligned block of 32 rows (0 to 31, 32 to 63, ..., all dimensions but the last counted through in order) at most 2 rows name the same one
- parent_slot: int32 [4, 196608], P('crop', 'scene'), may hold values from 0 to 63, as said below
- child_offset: int32 [4, 196608], P('crop', 'scene'), may hold values from 0 to 7, as said below
Outputs:
- fine_grad: bfloat16 [4, 196608, 128], P('crop', 'scene')
- down_grad: float32 [8, 128, 256], replicated
- up_grad: float32 [8, 256, 128], replicated
- bias_grad: float32 [256], replicated
The draws below stay inside these ranges and needn't reach their ends.
Inputs may be any that keep to these rules, and one draw needn't show every extreme that they name: `parent_slot`: within each aligned block of 192 fine sites the parent index never falls and each of the 64 parents has 1 to 8 sites. `child_offset`: offsets strictly rise within one parent. `block_owner`: among the 32 blocks of one scene index no owner is named more than 2 times, a bound that some block reaches.
All inputs are finite; a program needn't handle non-finite values.
Results may differ from the reference program's by a relative error of at most 0.005.
Values may be sent and summed in bfloat16 or wider, within the bound.
A program may use at most 128 MiB of HBM per device.

```python
import math
import jax
import jax.numpy as jnp
import numpy as np
from jax import lax

C_IN = 128
C_OUT = 256
PB = 64
BR = 192
K = 32
CAPB = 2
BLOCKS = 1024
FINE = 196608
CROPS = 4
N_SCENE = 32


def child_layout(key):
    block_keys = jax.random.split(jax.random.fold_in(key, 11), CROPS * BLOCKS)

    def one_block(block_key):
        first_key, second_key = jax.random.split(block_key)
        shuffled = jax.random.permutation(first_key, 7 * PB)
        extra = (shuffled < BR - PB).astype(jnp.int32).reshape(PB, 7).sum(axis=1)
        counts = 1 + extra
        scores = jax.random.randint(second_key, (PB, 8), 0, 1 << 20) * 8 + jnp.arange(8, dtype=jnp.int32)[None, :]
        ranks = jnp.argsort(jnp.argsort(scores, axis=1), axis=1)
        chosen = (ranks < counts[:, None]).astype(jnp.int32).reshape(-1)
        position = jnp.cumsum(chosen) - 1
        target = jnp.where(chosen > 0, position, BR)
        identity = jnp.arange(PB * 8, dtype=jnp.int32)
        slot_ids = jnp.zeros((BR,), jnp.int32).at[target].set(identity, mode='drop')
        return (slot_ids // 8, slot_ids % 8)
    parents, offsets = jax.vmap(one_block)(block_keys)
    return (parents.reshape(CROPS, BLOCKS * BR), offsets.reshape(CROPS, BLOCKS * BR))


def draw_parent_slot(key, part):
    return child_layout(key)[0]


def draw_child_offset(key, part):
    return child_layout(key)[1]


def levels(rng, shape, cuts, smallest, top_value):
    def one(axis_at, parts):
        draws = jax.random.uniform(jax.random.fold_in(jax.random.fold_in(rng, 6), axis_at), (parts,), jnp.float32, smallest / len(cuts), top_value / len(cuts))
        return jnp.repeat(jnp.exp(draws), shape[axis_at] // parts).reshape((-1,) + (1,) * (len(shape) - axis_at - 1))

    level = one(*cuts[0])
    for cut in cuts[1:]:
        level = level * one(*cut)
    return level


def shared_out(key, own, number, rows, count, top, reach, lean):
    order = jax.random.permutation(key, count)
    crowded, common = load_shares(count, rows * top, reach, lean, True), load_shares(count, rows * top, reach, lean, False)
    places = jnp.arange(count)

    def named(sizes, rotation):
        used = int((sizes > 0).sum())
        fixed = max(1, used // 4)
        shifted = fixed + (places - fixed + rotation * (used - fixed)) % max(1, count - fixed)
        return jnp.zeros((count,), jnp.int32).at[order[jnp.where(places < fixed, places, shifted)]].set(jnp.asarray(sizes, jnp.int32))

    sizes = jnp.where(number % 4 == 0, named(crowded, number // 4), named(common, number - number // 4 - 1))
    mixed = jax.random.permutation(jax.random.fold_in(own, 3), count)
    donor, taker = mixed[0:count // 2 * 2:2], mixed[1:count // 2 * 2:2]
    margin = jnp.minimum(sizes[donor] - 1, reach - sizes[taker]) // 2
    margin = jnp.where((donor == order[0]) | (taker == order[0]) | (sizes[taker] == 0), 0, jnp.maximum(margin, 0))
    shifted = jax.random.randint(jax.random.fold_in(own, 4), (count // 2,), 0, 1 << 20) % (margin + 1)
    sizes = sizes.at[donor].add(-shifted).at[taker].add(shifted)
    members = jnp.searchsorted(jnp.cumsum(sizes), jnp.arange(rows * top), side="right").astype(jnp.int32)
    listing = members.reshape(top, rows).T
    listing = listing[jax.random.permutation(jax.random.fold_in(own, 1), rows)]
    rotation = jax.random.randint(jax.random.fold_in(own, 2), (rows, 1), 0, top)
    return jnp.take_along_axis(listing, (jnp.arange(top)[None, :] + rotation) % top, axis=1)


def load_shares(amount, total, most, skew, full):
    loads = [(1 << 20) // math.isqrt(grade ** skew) + 1 for grade in range(1, amount + 1)]
    largest = most if full else min(most, max(-(-total // amount), total * loads[0] // sum(loads)))
    least = 1 if total - largest >= amount - 1 else 0
    given, rest = [largest] + [least] * (amount - 1), total - largest - least * (amount - 1)
    while rest > 0:
        free = [i for i in range(1, amount) if given[i] < largest] or [i for i in range(1, amount) if given[i] < most]
        mass, budget = sum([loads[i] for i in free]), rest
        for i in free:
            addition = min(most - given[i], max(1, budget * loads[i] // mass), rest)
            given[i] = given[i] + addition
            rest = rest - addition
    return np.array(given)


def noise(rng, shape, deviation, reach, cuts=(), kind=jnp.bfloat16):
    drawn = deviation * jax.random.normal(rng, shape, jnp.float32)
    if cuts:
        drawn = drawn * levels(rng, shape, cuts, -0.22, 0.18)
    return jnp.clip(drawn, -reach, reach).astype(kind)


def setup_inputs(seed: int = 0) -> dict:
    key_of = jax.random.split(jax.random.key(seed), 10)
    fine_feats = noise(key_of[0], (CROPS, FINE, C_IN), 1.0, 6.0, ((0, 4), (1, 32)))
    out_grad = noise(key_of[1], (CROPS, FINE, C_IN), 1.0, 6.0, ((0, 4), (1, 32)))
    pre_act = noise(key_of[2], (CROPS, N_SCENE, N_SCENE, CAPB, PB, C_OUT), 1.0, 6.0, ((0, 4), (1, 32)))
    deep_grad = noise(key_of[3], (CROPS, N_SCENE, N_SCENE, CAPB, PB, C_OUT), 1.0, 6.0, ((0, 4), (1, 32)))
    down_weight = noise(key_of[4], (8, C_IN, C_OUT), (3 * C_IN) ** -0.5, 0.3125)
    up_weight = noise(key_of[5], (8, C_OUT, C_IN), C_OUT ** -0.5, 0.375)
    block_owner_keys = jax.random.split(jax.random.fold_in(key_of[6], 1), CROPS * BLOCKS // K)
    block_owner_turns = jax.random.permutation(jax.random.fold_in(key_of[6], 3), CROPS * BLOCKS // K)
    block_owner = jax.vmap(lambda own, number: shared_out(jax.random.fold_in(key_of[6], 2), own, number, K, N_SCENE, 1, CAPB, 2))(block_owner_keys, block_owner_turns).reshape((CROPS, BLOCKS, 1))
    parent_slot = draw_parent_slot(jax.random.fold_in(key_of[9], 71), 0)
    child_offset = draw_child_offset(jax.random.fold_in(key_of[9], 71), 0)
    return {"fine_feats": fine_feats, "out_grad": out_grad, "pre_act": pre_act, "deep_grad": deep_grad, "down_weight": down_weight, "up_weight": up_weight, "block_owner": block_owner, "parent_slot": parent_slot, "child_offset": child_offset}


def silu_parts(pre_value):
    pre_float = pre_value.astype(jnp.float32)
    sig_value = jax.nn.sigmoid(pre_float)
    return pre_float * sig_value, sig_value * (1.0 + pre_float * (1.0 - sig_value))


def reference(fine_feats, out_grad, pre_act, deep_grad, down_weight, up_weight, block_owner, parent_slot, child_offset):
    wu_mat = jnp.transpose(up_weight, (0, 2, 1)).reshape(8 * C_IN, C_OUT)
    wd_mat = jnp.transpose(down_weight, (2, 0, 1)).reshape(C_OUT, 8 * C_IN)
    earlier = jnp.arange(K)[None, :] < jnp.arange(K)[:, None]
    places = (parent_slot * 8 + child_offset).astype(jnp.int32)
    block_base = jnp.repeat(jnp.arange(K, dtype=jnp.int32) * (PB * 8), BR)
    up_sum = jnp.zeros((C_OUT, 8 * C_IN), jnp.float32)
    down_sum = jnp.zeros((8 * C_IN, C_OUT), jnp.float32)
    bias_sum = jnp.zeros((C_OUT,), jnp.float32)
    results = []
    for crop_index in range(CROPS):
        owners = block_owner[crop_index, :, 0].reshape(N_SCENE, K)
        same_owner = owners[:, :, None] == owners[:, None, :]
        slot_rank = jnp.sum(same_owner & earlier[None], axis=2).astype(jnp.int32)
        pre_crop = pre_act[crop_index]
        deep_crop = deep_grad[crop_index]

        def block_step(totals, inputs):
            up_acc, down_acc, bias_acc = totals
            source, owner_row, rank_row, feats, cotan, place_row = inputs
            parent_pre = pre_crop[owner_row, source, rank_row].reshape(K * PB, C_OUT)
            parent_deep = deep_crop[owner_row, source, rank_row].reshape(K * PB, C_OUT)
            flat_index = (block_base + place_row).astype(jnp.int32)
            feat_slots = jnp.zeros((K * PB * 8, C_IN), fine_feats.dtype).at[flat_index].set(feats).reshape(K * PB, 8 * C_IN)
            cot_slots = jnp.zeros((K * PB * 8, C_IN), out_grad.dtype).at[flat_index].set(cotan).reshape(K * PB, 8 * C_IN)
            act_value, slope_value = silu_parts(parent_pre)
            act_grad = parent_deep.astype(jnp.float32) + jnp.dot(cot_slots, wu_mat, preferred_element_type=jnp.float32)
            pre_grad = (act_grad * slope_value).astype(jnp.bfloat16)
            slot_grads = jnp.dot(pre_grad, wd_mat, preferred_element_type=jnp.float32).reshape(K * PB * 8, C_IN)
            fine_part = slot_grads[flat_index].astype(jnp.bfloat16)
            up_acc = up_acc + jnp.dot(act_value.astype(jnp.bfloat16).T, cot_slots, preferred_element_type=jnp.float32)
            down_acc = down_acc + jnp.dot(feat_slots.T, pre_grad, preferred_element_type=jnp.float32)
            bias_acc = bias_acc + jnp.sum(pre_grad.astype(jnp.float32), axis=0)
            return (up_acc, down_acc, bias_acc), fine_part

        inputs = (jnp.arange(N_SCENE, dtype=jnp.int32), owners, slot_rank,
                  fine_feats[crop_index].reshape(N_SCENE, K * BR, C_IN),
                  out_grad[crop_index].reshape(N_SCENE, K * BR, C_IN),
                  places[crop_index].reshape(N_SCENE, K * BR))
        (up_sum, down_sum, bias_sum), fine_all = lax.scan(block_step, (up_sum, down_sum, bias_sum), inputs)
        results.append(fine_all.reshape(FINE, C_IN))
    grad_scale = float(CROPS * FINE) ** -0.5
    up_grad = jnp.transpose((up_sum * grad_scale).reshape(C_OUT, 8, C_IN), (1, 0, 2))
    down_grad = (down_sum * grad_scale).reshape(8, C_IN, C_OUT)
    return jnp.stack(results), down_grad, up_grad, bias_sum * grad_scale
```

```python
import functools

import jax
import jax.numpy as jnp
from jax import lax
from jax.experimental import pallas as pl
from jax.experimental.pallas import tpu as pltpu
from jax.sharding import PartitionSpec as P

MESH = pl.DeviceIdType.MESH
BF16 = jnp.bfloat16
F32 = jnp.float32
NT = (((1,), (0,)), ((), ()))
TN = (((0,), (0,)), ((), ()))

CHIP_ORDER = (
    (2, 1), (1, 2), (2, 3), (3, 2), (2, 2), (2, 0), (0, 2),
    (1, 3), (3, 1), (1, 1), (3, 3), (1, 0), (0, 1), (3, 0), (0, 3),
)
UPFRONT = 2


def level_kernel(
    scale,
    owner_ref, pslot_ref, coff_ref, feats_hbm, cotan_hbm, pre_hbm, deep_hbm, wd_ref, wu_ref,
    fine_out, down_out, up_out, bias_out,
    tgt, feats, cotan, recv0, recv1, recv2, recv3, chosen, cot_s, feat_t, x_s, slope_s, act_t, pg_s, wu_s, wd_s, fine_s,
    quarter, rec_a, msg_b, rec_b, part, load_sem, own_sem, x_send, x_recv,
    a_send, a_recv, b_send, b_recv, c_send, c_recv, d_send, d_recv, store_sem,
):
    recv = (recv0, recv1, recv2, recv3)
    z = lax.axis_index("crop")
    me = lax.axis_index("scene")
    chip, core = me // 2, me % 2
    cx, cy = chip // 4, chip % 4
    m = z * 2 + core

    def plane_peer(dx, dy, dc):
        return (((cx + dx) % 4) * 4 + (cy + dy) % 4) * 2 + (core + dc) % 2

    def group_peer(d):
        other = (m + d) % 8
        return other, (other // 2, chip * 2 + other % 2)

    def chip_peer(d):
        other = (chip + d) % 16
        return other, (z, other * 2 + core)

    barrier = pltpu.get_barrier_semaphore()

    def greet_plane(d, carry):
        pl.semaphore_signal(barrier, inc=1, device_id=(z, (me + d) % 32), device_id_type=MESH)
        return carry

    def greet_crops(d, carry):
        for c in range(2):
            pl.semaphore_signal(
                barrier, inc=1, device_id=((z + d) % 4, chip * 2 + c), device_id_type=MESH
            )
        return carry

    lax.fori_loop(1, 32, greet_plane, 0)
    lax.fori_loop(1, 4, greet_crops, 0)
    pl.semaphore_wait(barrier, 37)

    def source(q):
        return (pre_hbm if q < 2 else deep_hbm), pl.ds((q % 2) * 128, 128)

    def send_to(q, peer):
        ref, lanes = source(q)
        pltpu.make_async_remote_copy(
            src_ref=ref.at[pl.ds(2 * peer, 2), :, lanes],
            dst_ref=recv[q].at[pl.ds(2 * me, 2)],
            send_sem=x_send.at[q],
            recv_sem=x_recv.at[q],
            device_id=(z, peer),
            device_id_type=MESH,
        ).start()

    def own_copy(q):
        ref, lanes = source(q)
        return pltpu.make_async_copy(
            ref.at[pl.ds(2 * me, 2), :, lanes], recv[q].at[pl.ds(2 * me, 2)], own_sem.at[q]
        )

    def start_round(q):
        def half(dc, carry):
            for dx, dy in CHIP_ORDER:
                send_to(q, plane_peer(dx, dy, dc))
            return carry

        lax.fori_loop(0, 2, half, 0)
        send_to(q, plane_peer(0, 0, 1))
        own_copy(q).start()

    def bytes_of_round(q, sem):
        half = recv[q].at[pl.ds(0, 62)]
        return pltpu.make_async_copy(half, half, sem.at[q])

    def wait_round(q):
        own_copy(q).wait()
        bytes_of_round(q, x_recv).wait()

    for q in range(UPFRONT):
        start_round(q)

    loads = [
        pltpu.make_async_copy(cotan_hbm, cotan, load_sem.at[0]),
        pltpu.make_async_copy(feats_hbm, feats, load_sem.at[1]),
    ]
    for load in loads:
        load.start()

    def rank_block(b, carry):
        owner = owner_ref[b]
        count = jnp.int32(0)
        for other in range(32):
            count += jnp.where((owner_ref[other] == owner) & (other < b), 1, 0)
        tgt[b] = jnp.minimum(owner * 2 + count, 63)
        return carry

    lax.fori_loop(0, 32, rank_block, 0)

    for k in range(8):
        wu_s[pl.ds(k * 128, 128), :] = wu_ref[k].astype(F32).T.astype(BF16)
        wd_s[:, pl.ds(k * 128, 128)] = wd_ref[k].astype(F32).T.astype(BF16)
    for load in loads:
        load.wait()

    def place_pair(i, carry):
        rows, cols = [], []
        lane = lax.broadcasted_iota(jnp.int32, (1, 128), 1)
        for g in range(3):
            row = pl.ds(i * 3 + g, 1)
            place = coff_ref[row, :] * 128 + pslot_ref[row, :]
            if g == 1:
                place = place + jnp.where(lane >= 64, 64, 0)
            elif g == 2:
                place = place + 64
            sub = lax.broadcasted_iota(jnp.int32, (1024, 128), 0)
            rows.append(jnp.where(sub == place, 1.0, 0.0).astype(BF16))
            column = jnp.broadcast_to(place.astype(F32), (128, 128)).T
            lanes = lax.broadcasted_iota(jnp.int32, (128, 128), 1).astype(F32)
            for k in range(8):
                chosen[pl.ds(i * 384 + g * 128, 128), pl.ds(k * 128, 128)] = jnp.where(
                    column == lanes + float(k * 128), 1.0, 0.0
                ).astype(BF16)
        sites = pl.ds(i * 384, 384)
        parents = pl.ds(i * 128, 128)
        chooser = jnp.concatenate(rows, axis=1)
        placed = jnp.dot(chooser, cotan[sites, :], preferred_element_type=F32).astype(BF16)
        for k in range(8):
            cot_s[parents, pl.ds(k * 128, 128)] = placed[k * 128 : (k + 1) * 128, :]
        turned = lax.dot_general(
            feats[sites, :], chosen[sites, :], TN, preferred_element_type=F32
        ).astype(BF16)
        for k in range(8):
            feat_t[pl.ds(k * 128, 128), parents] = turned[:, k * 128 : (k + 1) * 128]
        return carry

    lax.fori_loop(0, 16, place_pair, 0)

    def up_tile(i, carry):
        rows = pl.ds(i * 512, 512)
        x_s[rows, :] = jnp.dot(cot_s[rows, :], wu_s[...], preferred_element_type=F32)
        return carry

    lax.fori_loop(0, 4, up_tile, 0)

    def start_a(q):
        def step(d, carry):
            other, device = group_peer(d)
            pltpu.make_async_remote_copy(
                src_ref=quarter.at[q, other], dst_ref=rec_a.at[q, m],
                send_sem=a_send.at[q], recv_sem=a_recv.at[q],
                device_id=device, device_id_type=MESH,
            ).start()
            return carry

        lax.fori_loop(1, 8, step, 0)
        rec_a[q, m] = quarter[q, m]

    def bytes_of(ref, sem):
        return pltpu.make_async_copy(ref, ref, sem)

    def next_b(q):
        bytes_of(rec_a.at[q, pl.ds(0, 7)], a_recv.at[q]).wait()
        total = rec_a[q, 0]
        for other in range(1, 8):
            total += rec_a[q, other]
        for n in range(16):
            msg_b[q, n, 0:8] = total[n * 8 : (n + 1) * 8]
            msg_b[q, n, 8:16] = total[128:136]

        def step(d, carry):
            other, device = chip_peer(d)
            pltpu.make_async_remote_copy(
                src_ref=msg_b.at[q, other], dst_ref=rec_b.at[q, chip],
                send_sem=b_send.at[q], recv_sem=b_recv.at[q],
                device_id=device, device_id_type=MESH,
            ).start()
            return carry

        lax.fori_loop(1, 16, step, 0)
        rec_b[q, chip] = msg_b[q, chip]

    def next_c(q):
        bytes_of(rec_b.at[q, pl.ds(0, 15)], b_recv.at[q]).wait()
        total = rec_b[q, 0]
        for other in range(1, 16):
            total += rec_b[q, other]
        total = total * scale
        mine = pl.ds(pl.multiple_of(chip * 8, 8), 8)
        part[q, mine] = total[0:8]
        if q >= 2:
            bias_out[:, pl.ds((q % 2) * 128, 128)] = jnp.sum(total[8:16], axis=0, keepdims=True)

        def step(d, carry):
            _, device = chip_peer(d)
            pltpu.make_async_remote_copy(
                src_ref=part.at[q, mine], dst_ref=part.at[q, mine],
                send_sem=c_send.at[q], recv_sem=c_recv.at[q],
                device_id=device, device_id_type=MESH,
            ).start()
            return carry

        lax.fori_loop(1, 16, step, 0)

    def result(q, index):
        half = pl.ds((q % 2) * 128, 128)
        return up_out.at[index, half, :] if q < 2 else down_out.at[index, :, half]

    def own_result(q):
        return pltpu.make_async_copy(part.at[q], result(q, m), store_sem.at[q])

    def next_d(q):
        bytes_of(part.at[q, pl.ds(0, 120)], c_recv.at[q]).wait()

        def step(d, carry):
            _, device = group_peer(d)
            pltpu.make_async_remote_copy(
                src_ref=part.at[q], dst_ref=result(q, m),
                send_sem=d_send.at[q], recv_sem=d_recv.at[q],
                device_id=device, device_id_type=MESH,
            ).start()
            return carry

        lax.fori_loop(1, 8, step, 0)
        own_result(q).start()

    def finish(q):
        own_result(q).wait()
        seven = result(q, pl.ds(0, 7))
        bytes_of(seven, d_recv.at[q]).wait()
        bytes_of(seven, d_send.at[q]).wait()
        bytes_of(rec_a.at[q, pl.ds(0, 7)], a_send.at[q]).wait()
        bytes_of(rec_b.at[q, pl.ds(0, 15)], b_send.at[q]).wait()
        bytes_of(part.at[q, pl.ds(0, 120)], c_send.at[q]).wait()
        bytes_of_round(q, x_send).wait()

    def up_round(q):
        half = pl.ds((q % 2) * 128, 128)
        wait_round(q)

        def pair(i, carry):
            rows = pl.ds(i * 128, 128)
            pre = jnp.concatenate(
                [recv[q][tgt[2 * i]], recv[q][tgt[2 * i + 1]]], axis=0
            ).astype(F32)
            sig = jax.nn.sigmoid(pre)
            slope_s[rows, half] = sig * (1.0 + pre * (1.0 - sig))
            act_t[:, rows] = (pre * sig).T.astype(BF16)
            return carry

        lax.fori_loop(0, 16, pair, 0)

        def tile(i, carry):
            term = jnp.dot(
                act_t[...], cot_s[:, pl.ds(pl.multiple_of(i * 256, 256), 256)],
                preferred_element_type=F32,
            )
            quarter[q, 2 * i, 0:128] = term[:, 0:128]
            quarter[q, 2 * i + 1, 0:128] = term[:, 128:256]
            return carry

        lax.fori_loop(0, 4, tile, 0)
        for other in range(8):
            quarter[q, other, 128:136] = jnp.zeros((8, 128), F32)

    def down_round(q):
        half = pl.ds((q % 2) * 128, 128)
        wait_round(q)

        def pair(i, bias):
            rows = pl.ds(i * 128, 128)
            deep = jnp.concatenate(
                [recv[q][tgt[2 * i]], recv[q][tgt[2 * i + 1]]], axis=0
            ).astype(F32)
            grad = ((deep + x_s[rows, half]) * slope_s[rows, half]).astype(BF16)
            pg_s[rows, half] = grad
            return bias + jnp.sum(grad.astype(F32).reshape(16, 8, 128), axis=0)

        bias = lax.fori_loop(0, 16, pair, jnp.zeros((8, 128), F32))

        def tile(i, carry):
            term = jnp.dot(
                feat_t[pl.ds(i * 256, 256), :], pg_s[:, half], preferred_element_type=F32
            )
            quarter[q, 2 * i, 0:128] = term[0:128]
            quarter[q, 2 * i + 1, 0:128] = term[128:256]
            return carry

        lax.fori_loop(0, 4, tile, 0)
        for other in range(8):
            quarter[q, other, 128:136] = bias

    def fine_rows(first, last):
        def pair(i, carry):
            grads = jnp.dot(
                pg_s[pl.ds(i * 128, 128), :], wd_s[...], preferred_element_type=F32
            ).astype(BF16)
            stacked = jnp.concatenate(
                [grads[:, k * 128 : (k + 1) * 128] for k in range(8)], axis=0
            )
            sites = pl.ds(i * 384, 384)
            fine_s[sites, :] = jnp.dot(
                chosen[sites, :], stacked, preferred_element_type=F32
            ).astype(BF16)
            return carry

        lax.fori_loop(first, last, pair, 0)

    def fine_copy():
        return pltpu.make_async_copy(fine_s, fine_out, store_sem.at[4])

    up_round(0)
    start_a(0)
    start_round(2)
    next_b(0)
    up_round(1)
    start_a(1)
    start_round(3)
    next_c(0)
    next_d(0)
    next_b(1)
    down_round(2)
    start_a(2)
    next_c(1)
    next_b(2)
    next_d(1)
    down_round(3)
    start_a(3)
    next_c(2)
    fine_rows(0, 6)
    next_b(3)
    next_d(2)
    fine_rows(6, 11)
    next_c(3)
    fine_rows(11, 16)
    fine_copy().start()
    next_d(3)
    for q in range(4):
        finish(q)
    fine_copy().wait()


def on_device(
    fine_feats, out_grad, pre_act, deep_grad, down_weight, up_weight,
    block_owner, parent_slot, child_offset,
):
    devices = lax.axis_size("scene") * lax.axis_size("crop")
    sites = fine_feats.shape[1]
    scale = float(devices * sites) ** (-0.5)
    hbm = pl.BlockSpec(memory_space=pl.ANY)
    vmem = pl.BlockSpec(memory_space=pltpu.VMEM)
    dma = pltpu.SemaphoreType.DMA
    call = pl.pallas_call(
        functools.partial(level_kernel, scale),
        out_shape=(
            jax.ShapeDtypeStruct((sites, 128), BF16),
            jax.ShapeDtypeStruct((8, 128, 256), F32),
            jax.ShapeDtypeStruct((8, 256, 128), F32),
            jax.ShapeDtypeStruct((1, 256), F32),
        ),
        in_specs=[
            pl.BlockSpec(memory_space=pltpu.SMEM), vmem, vmem, hbm, hbm, hbm, hbm, vmem, vmem,
        ],
        out_specs=(hbm, hbm, hbm, vmem),
        scratch_shapes=[
            pltpu.SMEM((32,), jnp.int32),
            pltpu.VMEM((sites, 128), BF16),
            pltpu.VMEM((sites, 128), BF16),
            pltpu.VMEM((64, 64, 128), BF16),
            pltpu.VMEM((64, 64, 128), BF16),
            pltpu.VMEM((64, 64, 128), BF16),
            pltpu.VMEM((64, 64, 128), BF16),
            pltpu.VMEM((sites, 1024), BF16),
            pltpu.VMEM((2048, 1024), BF16),
            pltpu.VMEM((1024, 2048), BF16),
            pltpu.VMEM((2048, 256), F32),
            pltpu.VMEM((2048, 256), F32),
            pltpu.VMEM((128, 2048), BF16),
            pltpu.VMEM((2048, 256), BF16),
            pltpu.VMEM((1024, 256), BF16),
            pltpu.VMEM((256, 1024), BF16),
            pltpu.VMEM((sites, 128), BF16),
            pltpu.VMEM((4, 8, 136, 128), F32),
            pltpu.VMEM((4, 8, 136, 128), F32),
            pltpu.VMEM((4, 16, 16, 128), F32),
            pltpu.VMEM((4, 16, 16, 128), F32),
            pltpu.VMEM((4, 128, 128), F32),
            dma((2,)), dma((4,)), dma((4,)), dma((4,)),
            dma((4,)), dma((4,)), dma((4,)), dma((4,)),
            dma((4,)), dma((4,)), dma((4,)), dma((4,)), dma((5,)),
        ],
        compiler_params=pltpu.CompilerParams(
            collective_id=0, has_side_effects=True, vmem_limit_bytes=60 << 20
        ),
        cost_estimate=pl.CostEstimate(
            flops=12 * 10**9, bytes_accessed=16 * 10**6, transcendentals=10**6
        ),
    )
    fine, down, up, bias = call(
        block_owner.reshape(32),
        parent_slot.reshape(sites // 128, 128),
        child_offset.reshape(sites // 128, 128),
        fine_feats[0],
        out_grad[0],
        pre_act.reshape(64, 64, 256),
        deep_grad.reshape(64, 64, 256),
        down_weight,
        up_weight,
    )
    return fine[None], down, up, bias[0]


def solution(mesh):
    return jax.shard_map(
        on_device,
        mesh=mesh,
        in_specs=(
            P("crop", "scene", None),
            P("crop", "scene", None),
            P("crop", "scene", None, None, None, None),
            P("crop", "scene", None, None, None, None),
            P(),
            P(),
            P("crop", "scene", None),
            P("crop", "scene"),
            P("crop", "scene"),
        ),
        out_specs=(P("crop", "scene", None), P(), P(), P()),
        check_vma=False,
    )
```

```python
import functools

import jax
import jax.numpy as jnp
from jax import lax
from jax.experimental import pallas as pl
from jax.experimental.pallas import tpu as pltpu
from jax.sharding import PartitionSpec as P

MESH = pl.DeviceIdType.MESH
BF16 = jnp.bfloat16
F32 = jnp.float32
TN = (((0,), (0,)), ((), ()))

CHIP_ORDER = (
    (2, 1), (1, 2), (2, 3), (3, 2), (2, 2), (2, 0), (0, 2),
    (1, 3), (3, 1), (1, 1), (3, 3), (1, 0), (0, 1), (3, 0), (0, 3),
)
UPFRONT = 4


def level_kernel(
    scale,
    owner_ref, pslot_ref, coff_ref, feats_hbm, cotan_hbm, pre_hbm, deep_hbm, wd_ref, wu_ref,
    fine_out, down_out, up_out, bias_out,
    tgt, feats, cotan, recv0, recv1, recv2, recv3, chosen, cot_t, feat_t, x_s, slope_s, act_s, pg_s, wd_s, fine_s,
    quarter, rec_a, msg_b, rec_b, part, rec_d, result, load_sem, own_sem, x_send, x_recv,
    a_send, a_recv, b_send, b_recv, c_send, c_recv, d_send, d_recv, store_sem,
):
    recv = (recv0, recv1, recv2, recv3)
    z = lax.axis_index("crop")
    me = lax.axis_index("scene")
    chip, core = me // 2, me % 2
    cx, cy = chip // 4, chip % 4
    m = z * 2 + core

    def plane_peer(dx, dy, dc):
        return (((cx + dx) % 4) * 4 + (cy + dy) % 4) * 2 + (core + dc) % 2

    def group_peer(d):
        other = (m + d) % 8
        return other, (other // 2, chip * 2 + other % 2)

    def chip_peer(d):
        other = (chip + d) % 16
        return other, (z, other * 2 + core)

    barrier = pltpu.get_barrier_semaphore()

    def greet_plane(d, carry):
        pl.semaphore_signal(barrier, inc=1, device_id=(z, (me + d) % 32), device_id_type=MESH)
        return carry

    def greet_crops(d, carry):
        for c in range(2):
            pl.semaphore_signal(
                barrier, inc=1, device_id=((z + d) % 4, chip * 2 + c), device_id_type=MESH
            )
        return carry

    lax.fori_loop(1, 32, greet_plane, 0)
    lax.fori_loop(1, 4, greet_crops, 0)
    pl.semaphore_wait(barrier, 37)

    def source(q):
        return (pre_hbm if q < 2 else deep_hbm), pl.ds((q % 2) * 128, 128)

    def send_to(q, peer):
        ref, lanes = source(q)
        pltpu.make_async_remote_copy(
            src_ref=ref.at[pl.ds(2 * peer, 2), :, lanes],
            dst_ref=recv[q].at[pl.ds(2 * me, 2)],
            send_sem=x_send.at[q],
            recv_sem=x_recv.at[q],
            device_id=(z, peer),
            device_id_type=MESH,
        ).start()

    def own_copy(q):
        ref, lanes = source(q)
        return pltpu.make_async_copy(
            ref.at[pl.ds(2 * me, 2), :, lanes], recv[q].at[pl.ds(2 * me, 2)], own_sem.at[q]
        )

    def start_round(q):
        def half(dc, carry):
            for dx, dy in CHIP_ORDER:
                send_to(q, plane_peer(dx, dy, dc))
            return carry

        lax.fori_loop(0, 2, half, 0)
        send_to(q, plane_peer(0, 0, 1))
        own_copy(q).start()

    def bytes_of_round(q, sem):
        half = recv[q].at[pl.ds(0, 62)]
        return pltpu.make_async_copy(half, half, sem.at[q])

    def wait_round(q):
        own_copy(q).wait()
        bytes_of_round(q, x_recv).wait()

    for q in range(UPFRONT):
        start_round(q)

    loads = [
        pltpu.make_async_copy(cotan_hbm, cotan, load_sem.at[0]),
        pltpu.make_async_copy(feats_hbm, feats, load_sem.at[1]),
    ]
    for load in loads:
        load.start()

    def rank_block(b, carry):
        owner = owner_ref[b]
        count = jnp.int32(0)
        for other in range(32):
            count += jnp.where((owner_ref[other] == owner) & (other < b), 1, 0)
        tgt[b] = jnp.minimum(owner * 2 + count, 63)
        return carry

    lax.fori_loop(0, 32, rank_block, 0)

    for k in range(8):
        wd_s[:, pl.ds(k * 128, 128)] = wd_ref[k].astype(F32).T.astype(BF16)
    for load in loads:
        load.wait()

    def place_pair(i, carry):
        for g in range(3):
            row = pl.ds(i * 3 + g, 1)
            place = (coff_ref[row, :] * 64 + pslot_ref[row, :]).astype(F32)
            column = jnp.broadcast_to(place, (128, 128)).T
            lanes = lax.broadcasted_iota(jnp.int32, (128, 128), 1).astype(F32)
            for k in range(4):
                chosen[pl.ds(i * 384 + g * 128, 128), pl.ds(k * 128, 128)] = jnp.where(
                    column == lanes + float(k * 128), 1.0, 0.0
                ).astype(BF16)
        turned = []
        for half in range(2):
            sites = pl.ds(i * 384 + half * 192, 192)
            both = jnp.concatenate([feats[sites, :], cotan[sites, :]], axis=1)
            turned.append(
                lax.dot_general(
                    both, chosen[sites, :], TN, preferred_element_type=F32
                ).astype(BF16)
            )
        parents = pl.ds(i * 128, 128)
        for k in range(8):
            rows, lanes = pl.ds(k * 128, 128), slice(k * 64, (k + 1) * 64)
            tile = jnp.concatenate([turned[0][:, lanes], turned[1][:, lanes]], axis=1)
            feat_t[rows, parents] = tile[0:128]
            cot_t[rows, parents] = tile[128:256]
        return carry

    lax.fori_loop(0, 16, place_pair, 0)

    wu_t = jnp.concatenate([wu_ref[k] for k in range(8)], axis=1)

    def up_tile(i, carry):
        rows = pl.ds(pl.multiple_of(i * 256, 256), 256)
        x_s[rows, :] = jnp.dot(wu_t, cot_t[:, rows], preferred_element_type=F32).T
        return carry

    lax.fori_loop(0, 8, up_tile, 0)

    def start_a(q):
        def step(d, carry):
            other, device = group_peer(d)
            pltpu.make_async_remote_copy(
                src_ref=quarter.at[q, other], dst_ref=rec_a.at[q, m],
                send_sem=a_send.at[q], recv_sem=a_recv.at[q],
                device_id=device, device_id_type=MESH,
            ).start()
            return carry

        lax.fori_loop(1, 8, step, 0)
        rec_a[q, m] = quarter[q, m]

    def bytes_of(ref, sem):
        return pltpu.make_async_copy(ref, ref, sem)

    def next_b(q):
        bytes_of(rec_a.at[q, pl.ds(0, 7)], a_recv.at[q]).wait()
        total = rec_a[q, 0].astype(F32)
        for other in range(1, 8):
            total += rec_a[q, other].astype(F32)
        bias = total[128:136] + total[136:144]
        for n in range(16):
            msg_b[q, n, 0:8] = total[n * 8 : (n + 1) * 8]
            msg_b[q, n, 8:16] = bias

        def step(d, carry):
            other, device = chip_peer(d)
            pltpu.make_async_remote_copy(
                src_ref=msg_b.at[q, other], dst_ref=rec_b.at[q, chip],
                send_sem=b_send.at[q], recv_sem=b_recv.at[q],
                device_id=device, device_id_type=MESH,
            ).start()
            return carry

        lax.fori_loop(1, 16, step, 0)
        rec_b[q, chip] = msg_b[q, chip]

    def next_c(q):
        bytes_of(rec_b.at[q, pl.ds(0, 15)], b_recv.at[q]).wait()
        total = rec_b[q, 0]
        for other in range(1, 16):
            total += rec_b[q, other]
        total = total * scale
        mine = pl.ds(pl.multiple_of(chip * 8, 8), 8)
        part[q, mine] = total[0:8]
        if q >= 2:
            bias_out[:, pl.ds((q % 2) * 128, 128)] = jnp.sum(total[8:16], axis=0, keepdims=True)

        def step(d, carry):
            _, device = chip_peer(d)
            pltpu.make_async_remote_copy(
                src_ref=part.at[q, mine], dst_ref=part.at[q, mine],
                send_sem=c_send.at[q], recv_sem=c_recv.at[q],
                device_id=device, device_id_type=MESH,
            ).start()
            return carry

        lax.fori_loop(1, 16, step, 0)

    def next_d(q):
        bytes_of(part.at[q, pl.ds(0, 120)], c_recv.at[q]).wait()
        block = part[q].T if q < 2 else part[q]
        rec_d[q, m] = block.astype(BF16)

        def step(d, carry):
            _, device = group_peer(d)
            pltpu.make_async_remote_copy(
                src_ref=rec_d.at[q, m], dst_ref=rec_d.at[q, m],
                send_sem=d_send.at[q], recv_sem=d_recv.at[q],
                device_id=device, device_id_type=MESH,
            ).start()
            return carry

        lax.fori_loop(1, 8, step, 0)

    def store_copy(q):
        half = pl.ds((q % 2) * 128, 128)
        target = up_out.at[:, half, :] if q < 2 else down_out.at[:, :, half]
        return pltpu.make_async_copy(result.at[q], target, store_sem.at[q])

    def store(q):
        bytes_of(rec_d.at[q, pl.ds(0, 7)], d_recv.at[q]).wait()
        result[q] = rec_d[q].astype(F32)
        store_copy(q).start()

    def finish(q):
        store_copy(q).wait()
        bytes_of(rec_d.at[q, pl.ds(0, 7)], d_send.at[q]).wait()
        bytes_of(rec_a.at[q, pl.ds(0, 7)], a_send.at[q]).wait()
        bytes_of(rec_b.at[q, pl.ds(0, 15)], b_send.at[q]).wait()
        bytes_of(part.at[q, pl.ds(0, 120)], c_send.at[q]).wait()
        bytes_of_round(q, x_send).wait()

    def products(q, left, right):
        def tile(i, carry):
            term = jnp.dot(left[pl.ds(i * 256, 256), :], right, preferred_element_type=F32)
            quarter[q, 2 * i, 0:128] = term[0:128].astype(BF16)
            quarter[q, 2 * i + 1, 0:128] = term[128:256].astype(BF16)
            return carry

        lax.fori_loop(0, 4, tile, 0)

    def up_round(q):
        half = pl.ds((q % 2) * 128, 128)
        wait_round(q)

        def pair(i, carry):
            rows = pl.ds(i * 128, 128)
            pre = jnp.concatenate(
                [recv[q][tgt[2 * i]], recv[q][tgt[2 * i + 1]]], axis=0
            ).astype(F32)
            sig = jax.nn.sigmoid(pre)
            slope_s[rows, half] = sig * (1.0 + pre * (1.0 - sig))
            act_s[rows, :] = (pre * sig).astype(BF16)
            return carry

        lax.fori_loop(0, 16, pair, 0)

        products(q, cot_t, act_s[...])
        for other in range(8):
            quarter[q, other, 128:144] = jnp.zeros((16, 128), BF16)

    def down_round(q):
        half = pl.ds((q % 2) * 128, 128)
        wait_round(q)

        def pair(i, bias):
            rows = pl.ds(i * 128, 128)
            deep = jnp.concatenate(
                [recv[q][tgt[2 * i]], recv[q][tgt[2 * i + 1]]], axis=0
            ).astype(F32)
            grad = ((deep + x_s[rows, half]) * slope_s[rows, half]).astype(BF16)
            pg_s[rows, half] = grad
            return bias + jnp.sum(grad.astype(F32).reshape(8, 16, 128), axis=0)

        bias = lax.fori_loop(0, 16, pair, jnp.zeros((16, 128), F32))

        products(q, feat_t, pg_s[:, half])
        for other in range(8):
            quarter[q, other, 128:144] = bias.astype(BF16)

    def fine_rows(first, last):
        def four(i, carry):
            grads = jnp.dot(
                pg_s[pl.ds(i * 256, 256), :], wd_s[...], preferred_element_type=F32
            ).astype(BF16)
            for j in range(4):
                stacked = jnp.concatenate(
                    [grads[j * 64 : (j + 1) * 64, k * 128 : (k + 1) * 128] for k in range(8)],
                    axis=0,
                )
                sites = pl.ds(i * 768 + j * 192, 192)
                fine_s[sites, :] = jnp.dot(
                    chosen[sites, :], stacked, preferred_element_type=F32
                ).astype(BF16)
            return carry

        lax.fori_loop(first, last, four, 0)

    def fine_copy():
        return pltpu.make_async_copy(fine_s, fine_out, store_sem.at[4])

    up_round(0)
    start_a(0)
    up_round(1)
    start_a(1)
    down_round(2)
    start_a(2)
    next_b(0)
    next_b(1)
    down_round(3)
    start_a(3)
    next_c(0)
    next_c(1)
    next_b(2)
    fine_rows(0, 2)
    next_b(3)
    next_c(2)
    next_d(0)
    next_d(1)
    fine_rows(2, 4)
    next_c(3)
    store(0)
    next_d(2)
    store(1)
    fine_rows(4, 6)
    next_d(3)
    store(2)
    fine_rows(6, 8)
    fine_copy().start()
    store(3)
    for q in range(4):
        finish(q)
    fine_copy().wait()


def on_device(
    fine_feats, out_grad, pre_act, deep_grad, down_weight, up_weight,
    block_owner, parent_slot, child_offset,
):
    devices = lax.axis_size("scene") * lax.axis_size("crop")
    sites = fine_feats.shape[1]
    scale = float(devices * sites) ** (-0.5)
    hbm = pl.BlockSpec(memory_space=pl.ANY)
    vmem = pl.BlockSpec(memory_space=pltpu.VMEM)
    dma = pltpu.SemaphoreType.DMA
    call = pl.pallas_call(
        functools.partial(level_kernel, scale),
        out_shape=(
            jax.ShapeDtypeStruct((sites, 128), BF16),
            jax.ShapeDtypeStruct((8, 128, 256), F32),
            jax.ShapeDtypeStruct((8, 256, 128), F32),
            jax.ShapeDtypeStruct((1, 256), F32),
        ),
        in_specs=[
            pl.BlockSpec(memory_space=pltpu.SMEM), vmem, vmem, hbm, hbm, hbm, hbm, vmem, vmem,
        ],
        out_specs=(hbm, hbm, hbm, vmem),
        scratch_shapes=[
            pltpu.SMEM((32,), jnp.int32),
            pltpu.VMEM((sites, 128), BF16),
            pltpu.VMEM((sites, 128), BF16),
            pltpu.VMEM((64, 64, 128), BF16),
            pltpu.VMEM((64, 64, 128), BF16),
            pltpu.VMEM((64, 64, 128), BF16),
            pltpu.VMEM((64, 64, 128), BF16),
            pltpu.VMEM((sites, 512), BF16),
            pltpu.VMEM((1024, 2048), BF16),
            pltpu.VMEM((1024, 2048), BF16),
            pltpu.VMEM((2048, 256), F32),
            pltpu.VMEM((2048, 256), F32),
            pltpu.VMEM((2048, 128), BF16),
            pltpu.VMEM((2048, 256), BF16),
            pltpu.VMEM((256, 1024), BF16),
            pltpu.VMEM((sites, 128), BF16),
            pltpu.VMEM((4, 8, 144, 128), BF16),
            pltpu.VMEM((4, 8, 144, 128), BF16),
            pltpu.VMEM((4, 16, 16, 128), F32),
            pltpu.VMEM((4, 16, 16, 128), F32),
            pltpu.VMEM((4, 128, 128), F32),
            pltpu.VMEM((4, 8, 128, 128), BF16),
            pltpu.VMEM((4, 8, 128, 128), F32),
            dma((2,)), dma((4,)), dma((4,)), dma((4,)),
            dma((4,)), dma((4,)), dma((4,)), dma((4,)),
            dma((4,)), dma((4,)), dma((4,)), dma((4,)), dma((5,)),
        ],
        compiler_params=pltpu.CompilerParams(
            collective_id=0, has_side_effects=True, vmem_limit_bytes=60 << 20
        ),
        cost_estimate=pl.CostEstimate(
            flops=12 * 10**9, bytes_accessed=16 * 10**6, transcendentals=10**6
        ),
    )
    fine, down, up, bias = call(
        block_owner.reshape(32),
        parent_slot.reshape(sites // 128, 128),
        child_offset.reshape(sites // 128, 128),
        fine_feats[0],
        out_grad[0],
        pre_act.reshape(64, 64, 256),
        deep_grad.reshape(64, 64, 256),
        down_weight,
        up_weight,
    )
    return fine[None], down, up, bias[0]


def solution(mesh):
    return jax.shard_map(
        on_device,
        mesh=mesh,
        in_specs=(
            P("crop", "scene", None),
            P("crop", "scene", None),
            P("crop", "scene", None, None, None, None),
            P("crop", "scene", None, None, None, None),
            P(),
            P(),
            P("crop", "scene", None),
            P("crop", "scene"),
            P("crop", "scene"),
        ),
        out_specs=(P("crop", "scene", None), P(), P(), P()),
        check_vma=False,
    )
```

```python
import functools

import jax
import jax.numpy as jnp
from jax import lax
from jax.experimental import pallas as pl
from jax.experimental.pallas import tpu as pltpu
from jax.sharding import PartitionSpec as P

MESH = pl.DeviceIdType.MESH
BF16 = jnp.bfloat16
F32 = jnp.float32
TN = (((0,), (0,)), ((), ()))

CHIP_ORDER = (
    (2, 1), (1, 2), (2, 3), (3, 2), (2, 2), (2, 0), (0, 2),
    (1, 3), (3, 1), (1, 1), (3, 3), (1, 0), (0, 1), (3, 0), (0, 3),
)
UPFRONT = 4


def level_kernel(
    scale,
    owner_ref, pslot_hbm, coff_hbm, feats_hbm, cotan_hbm, pre_hbm, deep_hbm, wd_hbm, wu_hbm,
    fine_out, tiles_out, bias_out,
    tgt, pslot_ref, coff_ref, wd_ref, wu_ref, feats, cotan, recv0, recv1, recv2, recv3, chosen, cot_t, feat_t, x_s, slope_s, act_s, pg_s, wd_s, fine_s,
    quarter, rec_a, msg_b, rec_b, part, mine_s, load_sem, own_sem, x_send, x_recv,
    a_send, a_recv, b_send, b_recv, c_send, c_recv, d_send, d_recv, store_sem,
):
    recv = (recv0, recv1, recv2, recv3)
    z = lax.axis_index("crop")
    me = lax.axis_index("scene")
    chip, core = me // 2, me % 2
    cx, cy = chip // 4, chip % 4
    m = z * 2 + core

    def plane_peer(dx, dy, dc):
        return (((cx + dx) % 4) * 4 + (cy + dy) % 4) * 2 + (core + dc) % 2

    def group_peer(d):
        other = (m + d) % 8
        return other, (other // 2, chip * 2 + other % 2)

    def chip_peer(d):
        other = (chip + d) % 16
        return other, (z, other * 2 + core)

    barrier = pltpu.get_barrier_semaphore()

    def greet_plane(d, carry):
        pl.semaphore_signal(barrier, inc=1, device_id=(z, (me + d) % 32), device_id_type=MESH)
        return carry

    def greet_crops(d, carry):
        for c in range(2):
            pl.semaphore_signal(
                barrier, inc=1, device_id=((z + d) % 4, chip * 2 + c), device_id_type=MESH
            )
        return carry

    lax.fori_loop(1, 32, greet_plane, 0)
    lax.fori_loop(1, 4, greet_crops, 0)
    pl.semaphore_wait(barrier, 37)

    def source(q):
        return (pre_hbm if q < 2 else deep_hbm), pl.ds((q % 2) * 128, 128)

    def send_to(q, peer):
        ref, lanes = source(q)
        pltpu.make_async_remote_copy(
            src_ref=ref.at[pl.ds(2 * peer, 2), :, lanes],
            dst_ref=recv[q].at[pl.ds(2 * me, 2)],
            send_sem=x_send.at[q],
            recv_sem=x_recv.at[q],
            device_id=(z, peer),
            device_id_type=MESH,
        ).start()

    def own_copy(q):
        ref, lanes = source(q)
        return pltpu.make_async_copy(
            ref.at[pl.ds(2 * me, 2), :, lanes], recv[q].at[pl.ds(2 * me, 2)], own_sem.at[q]
        )

    def start_round(q):
        def half(dc, carry):
            for dx, dy in CHIP_ORDER:
                send_to(q, plane_peer(dx, dy, dc))
            return carry

        lax.fori_loop(0, 2, half, 0)
        send_to(q, plane_peer(0, 0, 1))
        own_copy(q).start()

    def bytes_of_round(q, sem):
        half = recv[q].at[pl.ds(0, 62)]
        return pltpu.make_async_copy(half, half, sem.at[q])

    def wait_round(q):
        own_copy(q).wait()
        bytes_of_round(q, x_recv).wait()

    for q in range(UPFRONT):
        start_round(q)

    loads = [
        pltpu.make_async_copy(cotan_hbm, cotan, load_sem.at[0]),
        pltpu.make_async_copy(feats_hbm, feats, load_sem.at[1]),
        pltpu.make_async_copy(pslot_hbm, pslot_ref, load_sem.at[2]),
        pltpu.make_async_copy(coff_hbm, coff_ref, load_sem.at[3]),
        pltpu.make_async_copy(wd_hbm, wd_ref, load_sem.at[4]),
        pltpu.make_async_copy(wu_hbm, wu_ref, load_sem.at[5]),
    ]
    for load in loads:
        load.start()

    def rank_block(b, carry):
        owner = owner_ref[b]
        count = jnp.int32(0)
        for other in range(32):
            count += jnp.where((owner_ref[other] == owner) & (other < b), 1, 0)
        tgt[b] = jnp.minimum(owner * 2 + count, 63)
        return carry

    lax.fori_loop(0, 32, rank_block, 0)

    for load in loads:
        load.wait()
    for k in range(8):
        wd_s[:, pl.ds(k * 128, 128)] = wd_ref[k].astype(F32).T.astype(BF16)

    def place_pair(i, carry):
        for g in range(3):
            row = pl.ds(i * 3 + g, 1)
            place = (coff_ref[row, :] * 64 + pslot_ref[row, :]).astype(F32)
            column = jnp.broadcast_to(place, (128, 128)).T
            lanes = lax.broadcasted_iota(jnp.int32, (128, 128), 1).astype(F32)
            for k in range(4):
                chosen[pl.ds(i * 384 + g * 128, 128), pl.ds(k * 128, 128)] = jnp.where(
                    column == lanes + float(k * 128), 1.0, 0.0
                ).astype(BF16)
        turned = []
        for half in range(2):
            sites = pl.ds(i * 384 + half * 192, 192)
            both = jnp.concatenate([feats[sites, :], cotan[sites, :]], axis=1)
            turned.append(
                lax.dot_general(
                    both, chosen[sites, :], TN, preferred_element_type=F32
                ).astype(BF16)
            )
        parents = pl.ds(i * 128, 128)
        for k in range(8):
            rows, lanes = pl.ds(k * 128, 128), slice(k * 64, (k + 1) * 64)
            tile = jnp.concatenate([turned[0][:, lanes], turned[1][:, lanes]], axis=1)
            feat_t[rows, parents] = tile[0:128]
            cot_t[rows, parents] = tile[128:256]
        return carry

    lax.fori_loop(0, 16, place_pair, 0)

    wu_t = jnp.concatenate([wu_ref[k] for k in range(8)], axis=1)

    def up_tile(i, carry):
        rows = pl.ds(pl.multiple_of(i * 256, 256), 256)
        x_s[rows, :] = jnp.dot(wu_t, cot_t[:, rows], preferred_element_type=F32).T
        return carry

    lax.fori_loop(0, 8, up_tile, 0)

    def start_a(q):
        def step(d, carry):
            other, device = group_peer(d)
            pltpu.make_async_remote_copy(
                src_ref=quarter.at[q, other], dst_ref=rec_a.at[q, m],
                send_sem=a_send.at[q], recv_sem=a_recv.at[q],
                device_id=device, device_id_type=MESH,
            ).start()
            return carry

        lax.fori_loop(1, 8, step, 0)
        rec_a[q, m] = quarter[q, m]

    def bytes_of(ref, sem):
        return pltpu.make_async_copy(ref, ref, sem)

    def next_b(q):
        bytes_of(rec_a.at[q, pl.ds(0, 7)], a_recv.at[q]).wait()
        total = rec_a[q, 0].astype(F32)
        for other in range(1, 8):
            total += rec_a[q, other].astype(F32)
        bias = total[128:136] + total[136:144]
        for n in range(16):
            msg_b[q, n, 0:8] = total[n * 8 : (n + 1) * 8]
            msg_b[q, n, 8:16] = bias

        def step(d, carry):
            other, device = chip_peer(d)
            pltpu.make_async_remote_copy(
                src_ref=msg_b.at[q, other], dst_ref=rec_b.at[q, chip],
                send_sem=b_send.at[q], recv_sem=b_recv.at[q],
                device_id=device, device_id_type=MESH,
            ).start()
            return carry

        lax.fori_loop(1, 16, step, 0)
        rec_b[q, chip] = msg_b[q, chip]

    def next_c(q):
        bytes_of(rec_b.at[q, pl.ds(0, 15)], b_recv.at[q]).wait()
        total = rec_b[q, 0]
        for other in range(1, 16):
            total += rec_b[q, other]
        total = total * scale
        mine = pl.ds(pl.multiple_of(chip * 8, 8), 8)
        part[q, mine] = total[0:8]
        if q >= 2:
            bias_out[:, pl.ds((q % 2) * 128, 128)] = jnp.sum(total[8:16], axis=0, keepdims=True)

        def step(d, carry):
            _, device = chip_peer(d)
            pltpu.make_async_remote_copy(
                src_ref=part.at[q, mine], dst_ref=part.at[q, mine],
                send_sem=c_send.at[q], recv_sem=c_recv.at[q],
                device_id=device, device_id_type=MESH,
            ).start()
            return carry

        lax.fori_loop(1, 16, step, 0)

    def own_tile(q):
        return pltpu.make_async_copy(
            mine_s.at[q], tiles_out.at[q, m], store_sem.at[q]
        )

    def next_d(q):
        bytes_of(part.at[q, pl.ds(0, 120)], c_recv.at[q]).wait()
        block = part[q].T if q < 2 else part[q]
        mine_s[q] = block.astype(BF16)

        def step(d, carry):
            _, device = group_peer(d)
            pltpu.make_async_remote_copy(
                src_ref=mine_s.at[q], dst_ref=tiles_out.at[q, m],
                send_sem=d_send.at[q], recv_sem=d_recv.at[q],
                device_id=device, device_id_type=MESH,
            ).start()
            return carry

        lax.fori_loop(1, 8, step, 0)
        own_tile(q).start()

    def finish(q):
        own_tile(q).wait()
        seven = tiles_out.at[q, pl.ds(0, 7)]
        bytes_of(seven, d_recv.at[q]).wait()
        bytes_of(seven, d_send.at[q]).wait()
        bytes_of(rec_a.at[q, pl.ds(0, 7)], a_send.at[q]).wait()
        bytes_of(rec_b.at[q, pl.ds(0, 15)], b_send.at[q]).wait()
        bytes_of(part.at[q, pl.ds(0, 120)], c_send.at[q]).wait()
        bytes_of_round(q, x_send).wait()

    def products(q, left, right):
        def tile(i, carry):
            term = jnp.dot(left[pl.ds(i * 256, 256), :], right, preferred_element_type=F32)
            quarter[q, 2 * i, 0:128] = term[0:128].astype(BF16)
            quarter[q, 2 * i + 1, 0:128] = term[128:256].astype(BF16)
            return carry

        lax.fori_loop(0, 4, tile, 0)

    def up_round(q):
        half = pl.ds((q % 2) * 128, 128)
        wait_round(q)

        def pair(i, carry):
            rows = pl.ds(i * 128, 128)
            pre = jnp.concatenate(
                [recv[q][tgt[2 * i]], recv[q][tgt[2 * i + 1]]], axis=0
            ).astype(F32)
            sig = jax.nn.sigmoid(pre)
            slope_s[rows, half] = sig * (1.0 + pre * (1.0 - sig))
            act_s[rows, :] = (pre * sig).astype(BF16)
            return carry

        lax.fori_loop(0, 16, pair, 0)

        products(q, cot_t, act_s[...])
        for other in range(8):
            quarter[q, other, 128:144] = jnp.zeros((16, 128), BF16)

    def down_round(q):
        half = pl.ds((q % 2) * 128, 128)
        wait_round(q)

        def pair(i, bias):
            rows = pl.ds(i * 128, 128)
            deep = jnp.concatenate(
                [recv[q][tgt[2 * i]], recv[q][tgt[2 * i + 1]]], axis=0
            ).astype(F32)
            grad = ((deep + x_s[rows, half]) * slope_s[rows, half]).astype(BF16)
            pg_s[rows, half] = grad
            return bias + jnp.sum(grad.astype(F32).reshape(8, 16, 128), axis=0)

        bias = lax.fori_loop(0, 16, pair, jnp.zeros((16, 128), F32))

        products(q, feat_t, pg_s[:, half])
        for other in range(8):
            quarter[q, other, 128:144] = bias.astype(BF16)

    def fine_rows(first, last):
        def four(i, carry):
            grads = jnp.dot(
                pg_s[pl.ds(i * 256, 256), :], wd_s[...], preferred_element_type=F32
            ).astype(BF16)
            for j in range(4):
                stacked = jnp.concatenate(
                    [grads[j * 64 : (j + 1) * 64, k * 128 : (k + 1) * 128] for k in range(8)],
                    axis=0,
                )
                sites = pl.ds(i * 768 + j * 192, 192)
                fine_s[sites, :] = jnp.dot(
                    chosen[sites, :], stacked, preferred_element_type=F32
                ).astype(BF16)
            return carry

        lax.fori_loop(first, last, four, 0)

    def fine_copy():
        return pltpu.make_async_copy(fine_s, fine_out, store_sem.at[4])

    up_round(0)
    start_a(0)
    up_round(1)
    start_a(1)
    down_round(2)
    start_a(2)
    next_b(0)
    next_b(1)
    down_round(3)
    start_a(3)
    next_b(2)
    next_c(0)
    next_c(1)
    fine_rows(0, 2)
    next_b(3)
    next_d(0)
    next_d(1)
    next_c(2)
    fine_rows(2, 3)
    next_c(3)
    next_d(2)
    next_d(3)
    fine_rows(3, 8)
    fine_copy().start()
    for q in range(4):
        finish(q)
    fine_copy().wait()


def on_device(
    fine_feats, out_grad, pre_act, deep_grad, down_weight, up_weight,
    block_owner, parent_slot, child_offset,
):
    devices = lax.axis_size("scene") * lax.axis_size("crop")
    sites = fine_feats.shape[1]
    scale = float(devices * sites) ** (-0.5)
    hbm = pl.BlockSpec(memory_space=pl.ANY)
    vmem = pl.BlockSpec(memory_space=pltpu.VMEM)
    dma = pltpu.SemaphoreType.DMA
    call = pl.pallas_call(
        functools.partial(level_kernel, scale),
        out_shape=(
            jax.ShapeDtypeStruct((sites, 128), BF16),
            jax.ShapeDtypeStruct((4, 8, 128, 128), BF16),
            jax.ShapeDtypeStruct((1, 256), F32),
        ),
        in_specs=[
            pl.BlockSpec(memory_space=pltpu.SMEM), hbm, hbm, hbm, hbm, hbm, hbm, hbm, hbm,
        ],
        out_specs=(hbm, hbm, vmem),
        scratch_shapes=[
            pltpu.SMEM((32,), jnp.int32),
            pltpu.VMEM((sites // 128, 128), jnp.int32),
            pltpu.VMEM((sites // 128, 128), jnp.int32),
            pltpu.VMEM((8, 128, 256), BF16),
            pltpu.VMEM((8, 256, 128), BF16),
            pltpu.VMEM((sites, 128), BF16),
            pltpu.VMEM((sites, 128), BF16),
            pltpu.VMEM((64, 64, 128), BF16),
            pltpu.VMEM((64, 64, 128), BF16),
            pltpu.VMEM((64, 64, 128), BF16),
            pltpu.VMEM((64, 64, 128), BF16),
            pltpu.VMEM((sites, 512), BF16),
            pltpu.VMEM((1024, 2048), BF16),
            pltpu.VMEM((1024, 2048), BF16),
            pltpu.VMEM((2048, 256), F32),
            pltpu.VMEM((2048, 256), F32),
            pltpu.VMEM((2048, 128), BF16),
            pltpu.VMEM((2048, 256), BF16),
            pltpu.VMEM((256, 1024), BF16),
            pltpu.VMEM((sites, 128), BF16),
            pltpu.VMEM((4, 8, 144, 128), BF16),
            pltpu.VMEM((4, 8, 144, 128), BF16),
            pltpu.VMEM((4, 16, 16, 128), F32),
            pltpu.VMEM((4, 16, 16, 128), F32),
            pltpu.VMEM((4, 128, 128), F32),
            pltpu.VMEM((4, 128, 128), BF16),
            dma((6,)), dma((4,)), dma((4,)), dma((4,)),
            dma((4,)), dma((4,)), dma((4,)), dma((4,)),
            dma((4,)), dma((4,)), dma((4,)), dma((4,)), dma((5,)),
        ],
        compiler_params=pltpu.CompilerParams(
            collective_id=0, has_side_effects=True, vmem_limit_bytes=60 << 20
        ),
        cost_estimate=pl.CostEstimate(
            flops=12 * 10**9, bytes_accessed=16 * 10**6, transcendentals=10**6
        ),
    )
    fine, tiles, bias = call(
        block_owner.reshape(32),
        parent_slot.reshape(sites // 128, 128),
        child_offset.reshape(sites // 128, 128),
        fine_feats[0],
        out_grad[0],
        pre_act.reshape(64, 64, 256),
        deep_grad.reshape(64, 64, 256),
        down_weight,
        up_weight,
    )
    up = jnp.concatenate([tiles[0], tiles[1]], axis=1).astype(F32)
    down = jnp.concatenate([tiles[2], tiles[3]], axis=2).astype(F32)
    return fine[None], down, up, bias[0]


def solution(mesh):
    return jax.shard_map(
        on_device,
        mesh=mesh,
        in_specs=(
            P("crop", "scene", None),
            P("crop", "scene", None),
            P("crop", "scene", None, None, None, None),
            P("crop", "scene", None, None, None, None),
            P(),
            P(),
            P("crop", "scene", None),
            P("crop", "scene"),
            P("crop", "scene"),
        ),
        out_specs=(P("crop", "scene", None), P(), P(), P()),
        check_vma=False,
    )
```

```python
import functools

import jax
import jax.numpy as jnp
from jax import lax
from jax.experimental import pallas as pl
from jax.experimental.pallas import tpu as pltpu
from jax.sharding import PartitionSpec as P

MESH = pl.DeviceIdType.MESH
BF16 = jnp.bfloat16
F32 = jnp.float32
TN = (((0,), (0,)), ((), ()))

CHIP_ORDER = (
    (2, 2), (2, 1), (1, 2), (2, 3), (3, 2), (1, 1), (3, 3),
    (1, 3), (3, 1), (2, 0), (0, 2), (1, 0), (0, 1), (3, 0), (0, 3),
)
UPFRONT = 4


def level_kernel(
    scale,
    owner_ref, pslot_hbm, coff_hbm, feats_hbm, cotan_hbm, pre_hbm, deep_hbm, wd_hbm, wu_hbm,
    fine_out, tiles_out, bias_out,
    tgt, pslot_ref, coff_ref, wd_ref, wu_ref, feats, cotan, recv0, recv1, recv2, recv3, chosen, cot_t, feat_t, x_s, slope_s, act_s, pg_s, wd_s, fine_s,
    quarter, rec_a, msg_b, rec_b, part, mine_s, load_sem, own_sem, x_send, x_recv,
    a_send, a_recv, b_send, b_recv, c_send, c_recv, d_send, d_recv, store_sem,
):
    recv = (recv0, recv1, recv2, recv3)
    z = lax.axis_index("crop")
    me = lax.axis_index("scene")
    chip, core = me // 2, me % 2
    cx, cy = chip // 4, chip % 4
    m = z * 2 + core

    def plane_peer(dx, dy, dc):
        return (((cx + dx) % 4) * 4 + (cy + dy) % 4) * 2 + (core + dc) % 2

    def group_peer(d):
        other = (m + d) % 8
        return other, (other // 2, chip * 2 + other % 2)

    def chip_peer(d):
        other = (chip + d) % 16
        return other, (z, other * 2 + core)

    barrier = pltpu.get_barrier_semaphore()

    def greet_plane(d, carry):
        pl.semaphore_signal(barrier, inc=1, device_id=(z, (me + d) % 32), device_id_type=MESH)
        return carry

    def greet_crops(d, carry):
        for c in range(2):
            pl.semaphore_signal(
                barrier, inc=1, device_id=((z + d) % 4, chip * 2 + c), device_id_type=MESH
            )
        return carry

    lax.fori_loop(1, 32, greet_plane, 0)
    lax.fori_loop(1, 4, greet_crops, 0)
    pl.semaphore_wait(barrier, 37)

    def source(q):
        return (pre_hbm if q < 2 else deep_hbm), pl.ds((q % 2) * 128, 128)

    def send_to(q, peer):
        ref, lanes = source(q)
        pltpu.make_async_remote_copy(
            src_ref=ref.at[pl.ds(2 * peer, 2), :, lanes],
            dst_ref=recv[q].at[pl.ds(2 * me, 2)],
            send_sem=x_send.at[q],
            recv_sem=x_recv.at[q],
            device_id=(z, peer),
            device_id_type=MESH,
        ).start()

    def own_copy(q):
        ref, lanes = source(q)
        return pltpu.make_async_copy(
            ref.at[pl.ds(2 * me, 2), :, lanes], recv[q].at[pl.ds(2 * me, 2)], own_sem.at[q]
        )

    def start_round(q):
        def half(dc, carry):
            for dx, dy in CHIP_ORDER:
                send_to(q, plane_peer(dx, dy, dc))
            return carry

        lax.fori_loop(0, 2, half, 0)
        send_to(q, plane_peer(0, 0, 1))
        own_copy(q).start()

    def bytes_of_round(q, sem):
        half = recv[q].at[pl.ds(0, 62)]
        return pltpu.make_async_copy(half, half, sem.at[q])

    def wait_round(q):
        own_copy(q).wait()
        bytes_of_round(q, x_recv).wait()

    for q in range(UPFRONT):
        start_round(q)

    loads = [
        pltpu.make_async_copy(cotan_hbm, cotan, load_sem.at[0]),
        pltpu.make_async_copy(feats_hbm, feats, load_sem.at[1]),
        pltpu.make_async_copy(pslot_hbm, pslot_ref, load_sem.at[2]),
        pltpu.make_async_copy(coff_hbm, coff_ref, load_sem.at[3]),
        pltpu.make_async_copy(wd_hbm, wd_ref, load_sem.at[4]),
        pltpu.make_async_copy(wu_hbm, wu_ref, load_sem.at[5]),
    ]
    for load in loads:
        load.start()

    def rank_block(b, carry):
        owner = owner_ref[b]
        count = jnp.int32(0)
        for other in range(32):
            count += jnp.where((owner_ref[other] == owner) & (other < b), 1, 0)
        tgt[b] = jnp.minimum(owner * 2 + count, 63)
        return carry

    lax.fori_loop(0, 32, rank_block, 0)

    for load in loads:
        load.wait()
    for k in range(8):
        wd_s[:, pl.ds(k * 128, 128)] = wd_ref[k].astype(F32).T.astype(BF16)

    def place_pair(i, carry):
        for g in range(3):
            row = pl.ds(i * 3 + g, 1)
            place = (coff_ref[row, :] * 64 + pslot_ref[row, :]).astype(F32)
            column = jnp.broadcast_to(place, (128, 128)).T
            lanes = lax.broadcasted_iota(jnp.int32, (128, 128), 1).astype(F32)
            for k in range(4):
                chosen[pl.ds(i * 384 + g * 128, 128), pl.ds(k * 128, 128)] = jnp.where(
                    column == lanes + float(k * 128), 1.0, 0.0
                ).astype(BF16)
        turned = []
        for half in range(2):
            sites = pl.ds(i * 384 + half * 192, 192)
            both = jnp.concatenate([feats[sites, :], cotan[sites, :]], axis=1)
            turned.append(
                lax.dot_general(
                    both, chosen[sites, :], TN, preferred_element_type=F32
                ).astype(BF16)
            )
        parents = pl.ds(i * 128, 128)
        for k in range(8):
            rows, lanes = pl.ds(k * 128, 128), slice(k * 64, (k + 1) * 64)
            tile = jnp.concatenate([turned[0][:, lanes], turned[1][:, lanes]], axis=1)
            feat_t[rows, parents] = tile[0:128]
            cot_t[rows, parents] = tile[128:256]
        return carry

    lax.fori_loop(0, 16, place_pair, 0)

    wu_t = jnp.concatenate([wu_ref[k] for k in range(8)], axis=1)

    def up_tile(i, carry):
        rows = pl.ds(pl.multiple_of(i * 256, 256), 256)
        x_s[rows, :] = jnp.dot(wu_t, cot_t[:, rows], preferred_element_type=F32).T
        return carry

    lax.fori_loop(0, 8, up_tile, 0)

    def send_a(q, other):
        pltpu.make_async_remote_copy(
            src_ref=quarter.at[q, other], dst_ref=rec_a.at[q, m],
            send_sem=a_send.at[q], recv_sem=a_recv.at[q],
            device_id=(other // 2, chip * 2 + other % 2), device_id_type=MESH,
        ).start()

    def start_a(q):
        rec_a[q, m] = quarter[q, m]

    def bytes_of(ref, sem):
        return pltpu.make_async_copy(ref, ref, sem)

    def next_b(q):
        bytes_of(rec_a.at[q, pl.ds(0, 7)], a_recv.at[q]).wait()
        total = rec_a[q, 0].astype(F32)
        for other in range(1, 8):
            total += rec_a[q, other].astype(F32)
        bias = total[128:136] + total[136:144]
        for n in range(16):
            msg_b[q, n, 0:8] = total[n * 8 : (n + 1) * 8]
            msg_b[q, n, 8:16] = bias

        def step(d, carry):
            other, device = chip_peer(d)
            pltpu.make_async_remote_copy(
                src_ref=msg_b.at[q, other], dst_ref=rec_b.at[q, chip],
                send_sem=b_send.at[q], recv_sem=b_recv.at[q],
                device_id=device, device_id_type=MESH,
            ).start()
            return carry

        lax.fori_loop(1, 16, step, 0)
        rec_b[q, chip] = msg_b[q, chip]

    def next_c(q):
        bytes_of(rec_b.at[q, pl.ds(0, 15)], b_recv.at[q]).wait()
        total = rec_b[q, 0]
        for other in range(1, 16):
            total += rec_b[q, other]
        total = total * scale
        mine = pl.ds(pl.multiple_of(chip * 8, 8), 8)
        part[q, mine] = total[0:8]
        if q >= 2:
            bias_out[:, pl.ds((q % 2) * 128, 128)] = jnp.sum(total[8:16], axis=0, keepdims=True)

        def step(d, carry):
            _, device = chip_peer(d)
            pltpu.make_async_remote_copy(
                src_ref=part.at[q, mine], dst_ref=part.at[q, mine],
                send_sem=c_send.at[q], recv_sem=c_recv.at[q],
                device_id=device, device_id_type=MESH,
            ).start()
            return carry

        lax.fori_loop(1, 16, step, 0)

    def own_tile(q):
        return pltpu.make_async_copy(
            mine_s.at[q], tiles_out.at[q, m], store_sem.at[q]
        )

    def next_d(q):
        bytes_of(part.at[q, pl.ds(0, 120)], c_recv.at[q]).wait()
        block = part[q].T if q < 2 else part[q]
        mine_s[q] = block.astype(BF16)

        def step(d, carry):
            _, device = group_peer(d)
            pltpu.make_async_remote_copy(
                src_ref=mine_s.at[q], dst_ref=tiles_out.at[q, m],
                send_sem=d_send.at[q], recv_sem=d_recv.at[q],
                device_id=device, device_id_type=MESH,
            ).start()
            return carry

        lax.fori_loop(1, 8, step, 0)
        own_tile(q).start()

    def finish(q):
        own_tile(q).wait()
        seven = tiles_out.at[q, pl.ds(0, 7)]
        bytes_of(seven, d_recv.at[q]).wait()
        bytes_of(seven, d_send.at[q]).wait()
        bytes_of(rec_a.at[q, pl.ds(0, 7)], a_send.at[q]).wait()
        bytes_of(rec_b.at[q, pl.ds(0, 15)], b_send.at[q]).wait()
        bytes_of(part.at[q, pl.ds(0, 120)], c_send.at[q]).wait()
        bytes_of_round(q, x_send).wait()

    def products(q, left, right):
        def tile(i, carry):
            term = jnp.dot(left[pl.ds(i * 256, 256), :], right, preferred_element_type=F32)
            quarter[q, 2 * i, 0:128] = term[0:128].astype(BF16)
            quarter[q, 2 * i + 1, 0:128] = term[128:256].astype(BF16)
            for other in (2 * i, 2 * i + 1):
                @pl.when(other != m)
                def _():
                    send_a(q, other)
            return carry

        lax.fori_loop(0, 4, tile, 0)

    def up_round(q):
        half = pl.ds((q % 2) * 128, 128)
        wait_round(q)

        def pair(i, carry):
            rows = pl.ds(i * 128, 128)
            pre = jnp.concatenate(
                [recv[q][tgt[2 * i]], recv[q][tgt[2 * i + 1]]], axis=0
            ).astype(F32)
            sig = jax.nn.sigmoid(pre)
            slope_s[rows, half] = sig * (1.0 + pre * (1.0 - sig))
            act_s[rows, :] = (pre * sig).astype(BF16)
            return carry

        lax.fori_loop(0, 16, pair, 0)

        for other in range(8):
            quarter[q, other, 128:144] = jnp.zeros((16, 128), BF16)
        products(q, cot_t, act_s[...])

    def down_round(q):
        half = pl.ds((q % 2) * 128, 128)
        wait_round(q)

        def pair(i, bias):
            rows = pl.ds(i * 128, 128)
            deep = jnp.concatenate(
                [recv[q][tgt[2 * i]], recv[q][tgt[2 * i + 1]]], axis=0
            ).astype(F32)
            grad = ((deep + x_s[rows, half]) * slope_s[rows, half]).astype(BF16)
            pg_s[rows, half] = grad
            return bias + jnp.sum(grad.astype(F32).reshape(8, 16, 128), axis=0)

        bias = lax.fori_loop(0, 16, pair, jnp.zeros((16, 128), F32))

        for other in range(8):
            quarter[q, other, 128:144] = bias.astype(BF16)
        products(q, feat_t, pg_s[:, half])

    def fine_rows(first, last):
        def four(i, carry):
            grads = jnp.dot(
                pg_s[pl.ds(i * 256, 256), :], wd_s[...], preferred_element_type=F32
            ).astype(BF16)
            for j in range(4):
                stacked = jnp.concatenate(
                    [grads[j * 64 : (j + 1) * 64, k * 128 : (k + 1) * 128] for k in range(8)],
                    axis=0,
                )
                sites = pl.ds(i * 768 + j * 192, 192)
                fine_s[sites, :] = jnp.dot(
                    chosen[sites, :], stacked, preferred_element_type=F32
                ).astype(BF16)
            return carry

        lax.fori_loop(first, last, four, 0)

    def fine_copy():
        return pltpu.make_async_copy(fine_s, fine_out, store_sem.at[4])

    up_round(0)
    start_a(0)
    up_round(1)
    start_a(1)
    down_round(2)
    start_a(2)
    next_b(0)
    next_b(1)
    down_round(3)
    start_a(3)
    next_b(2)
    next_c(0)
    next_c(1)
    fine_rows(0, 2)
    next_b(3)
    next_d(0)
    next_d(1)
    next_c(2)
    fine_rows(2, 3)
    next_c(3)
    next_d(2)
    next_d(3)
    fine_rows(3, 8)
    fine_copy().start()
    for q in range(4):
        finish(q)
    fine_copy().wait()


def on_device(
    fine_feats, out_grad, pre_act, deep_grad, down_weight, up_weight,
    block_owner, parent_slot, child_offset,
):
    devices = lax.axis_size("scene") * lax.axis_size("crop")
    sites = fine_feats.shape[1]
    scale = float(devices * sites) ** (-0.5)
    hbm = pl.BlockSpec(memory_space=pl.ANY)
    vmem = pl.BlockSpec(memory_space=pltpu.VMEM)
    dma = pltpu.SemaphoreType.DMA
    call = pl.pallas_call(
        functools.partial(level_kernel, scale),
        out_shape=(
            jax.ShapeDtypeStruct((sites, 128), BF16),
            jax.ShapeDtypeStruct((4, 8, 128, 128), BF16),
            jax.ShapeDtypeStruct((1, 256), F32),
        ),
        in_specs=[
            pl.BlockSpec(memory_space=pltpu.SMEM), hbm, hbm, hbm, hbm, hbm, hbm, hbm, hbm,
        ],
        out_specs=(hbm, hbm, vmem),
        scratch_shapes=[
            pltpu.SMEM((32,), jnp.int32),
            pltpu.VMEM((sites // 128, 128), jnp.int32),
            pltpu.VMEM((sites // 128, 128), jnp.int32),
            pltpu.VMEM((8, 128, 256), BF16),
            pltpu.VMEM((8, 256, 128), BF16),
            pltpu.VMEM((sites, 128), BF16),
            pltpu.VMEM((sites, 128), BF16),
            pltpu.VMEM((64, 64, 128), BF16),
            pltpu.VMEM((64, 64, 128), BF16),
            pltpu.VMEM((64, 64, 128), BF16),
            pltpu.VMEM((64, 64, 128), BF16),
            pltpu.VMEM((sites, 512), BF16),
            pltpu.VMEM((1024, 2048), BF16),
            pltpu.VMEM((1024, 2048), BF16),
            pltpu.VMEM((2048, 256), F32),
            pltpu.VMEM((2048, 256), F32),
            pltpu.VMEM((2048, 128), BF16),
            pltpu.VMEM((2048, 256), BF16),
            pltpu.VMEM((256, 1024), BF16),
            pltpu.VMEM((sites, 128), BF16),
            pltpu.VMEM((4, 8, 144, 128), BF16),
            pltpu.VMEM((4, 8, 144, 128), BF16),
            pltpu.VMEM((4, 16, 16, 128), F32),
            pltpu.VMEM((4, 16, 16, 128), F32),
            pltpu.VMEM((4, 128, 128), F32),
            pltpu.VMEM((4, 128, 128), BF16),
            dma((6,)), dma((4,)), dma((4,)), dma((4,)),
            dma((4,)), dma((4,)), dma((4,)), dma((4,)),
            dma((4,)), dma((4,)), dma((4,)), dma((4,)), dma((5,)),
        ],
        compiler_params=pltpu.CompilerParams(
            collective_id=0, has_side_effects=True, vmem_limit_bytes=60 << 20
        ),
        cost_estimate=pl.CostEstimate(
            flops=12 * 10**9, bytes_accessed=16 * 10**6, transcendentals=10**6
        ),
    )
    fine, tiles, bias = call(
        block_owner.reshape(32),
        parent_slot.reshape(sites // 128, 128),
        child_offset.reshape(sites // 128, 128),
        fine_feats[0],
        out_grad[0],
        pre_act.reshape(64, 64, 256),
        deep_grad.reshape(64, 64, 256),
        down_weight,
        up_weight,
    )
    up = jnp.concatenate([tiles[0], tiles[1]], axis=1).astype(F32)
    down = jnp.concatenate([tiles[2], tiles[3]], axis=2).astype(F32)
    return fine[None], down, up, bias[0]


def solution(mesh):
    return jax.shard_map(
        on_device,
        mesh=mesh,
        in_specs=(
            P("crop", "scene", None),
            P("crop", "scene", None),
            P("crop", "scene", None, None, None, None),
            P("crop", "scene", None, None, None, None),
            P(),
            P(),
            P("crop", "scene", None),
            P("crop", "scene"),
            P("crop", "scene"),
        ),
        out_specs=(P("crop", "scene", None), P(), P(), P()),
        check_vma=False,
    )
```

```python
import functools

import jax
import jax.numpy as jnp
from jax import lax
from jax.experimental import pallas as pl
from jax.experimental.pallas import tpu as pltpu
from jax.sharding import PartitionSpec as P

MESH = pl.DeviceIdType.MESH
BF16 = jnp.bfloat16
F32 = jnp.float32
TN = (((0,), (0,)), ((), ()))

CHIP_ORDER = (
    (2, 2), (2, 1), (1, 2), (2, 3), (3, 2), (1, 1), (3, 3),
    (1, 3), (3, 1), (2, 0), (0, 2), (1, 0), (0, 1), (3, 0), (0, 3),
)
UPFRONT = 4


def level_kernel(
    scale,
    owner_ref, pslot_hbm, coff_hbm, feats_hbm, cotan_hbm, pre_hbm, deep_hbm, wd_hbm, wu_hbm,
    fine_out, tiles_out, bias_out,
    tgt, pslot_ref, coff_ref, wd_ref, wu_ref, feats, cotan, recv0, recv1, recv2, recv3, chosen, cot_t, feat_t, x_s, slope_s, act_s, pg_s, wd_s, fine_s,
    quarter, rec_a, msg_b, rec_b, part, mine_s, load_sem, own_sem, x_send, x_recv,
    a_send, a_recv, b_send, b_recv, c_send, c_recv, d_send, d_recv, store_sem,
):
    recv = (recv0, recv1, recv2, recv3)
    z = lax.axis_index("crop")
    me = lax.axis_index("scene")
    chip, core = me // 2, me % 2
    cx, cy = chip // 4, chip % 4
    m = z * 2 + core

    def plane_peer(dx, dy, dc):
        return (((cx + dx) % 4) * 4 + (cy + dy) % 4) * 2 + (core + dc) % 2

    def group_peer(d):
        other = (m + d) % 8
        return other, (other // 2, chip * 2 + other % 2)

    def chip_peer(d):
        other = (chip + d) % 16
        return other, (z, other * 2 + core)

    barrier = pltpu.get_barrier_semaphore()

    def greet_plane(d, carry):
        pl.semaphore_signal(barrier, inc=1, device_id=(z, (me + d) % 32), device_id_type=MESH)
        return carry

    def greet_crops(d, carry):
        for c in range(2):
            pl.semaphore_signal(
                barrier, inc=1, device_id=((z + d) % 4, chip * 2 + c), device_id_type=MESH
            )
        return carry

    lax.fori_loop(1, 32, greet_plane, 0)
    lax.fori_loop(1, 4, greet_crops, 0)
    pl.semaphore_wait(barrier, 37)

    def source(q):
        return (pre_hbm if q < 2 else deep_hbm), pl.ds((q % 2) * 128, 128)

    def send_to(q, peer):
        ref, lanes = source(q)
        pltpu.make_async_remote_copy(
            src_ref=ref.at[pl.ds(2 * peer, 2), :, lanes],
            dst_ref=recv[q].at[pl.ds(2 * me, 2)],
            send_sem=x_send.at[q],
            recv_sem=x_recv.at[q],
            device_id=(z, peer),
            device_id_type=MESH,
        ).start()

    def own_copy(q):
        ref, lanes = source(q)
        return pltpu.make_async_copy(
            ref.at[pl.ds(2 * me, 2), :, lanes], recv[q].at[pl.ds(2 * me, 2)], own_sem.at[q]
        )

    def start_round(q):
        def half(dc, carry):
            for dx, dy in CHIP_ORDER:
                send_to(q, plane_peer(dx, dy, dc))
            return carry

        lax.fori_loop(0, 2, half, 0)
        send_to(q, plane_peer(0, 0, 1))
        own_copy(q).start()

    def bytes_of_round(q, sem):
        half = recv[q].at[pl.ds(0, 62)]
        return pltpu.make_async_copy(half, half, sem.at[q])

    def wait_round(q):
        own_copy(q).wait()
        bytes_of_round(q, x_recv).wait()

    for q in range(UPFRONT):
        start_round(q)

    loads = [
        pltpu.make_async_copy(cotan_hbm, cotan, load_sem.at[0]),
        pltpu.make_async_copy(feats_hbm, feats, load_sem.at[1]),
        pltpu.make_async_copy(pslot_hbm, pslot_ref, load_sem.at[2]),
        pltpu.make_async_copy(coff_hbm, coff_ref, load_sem.at[3]),
        pltpu.make_async_copy(wd_hbm, wd_ref, load_sem.at[4]),
        pltpu.make_async_copy(wu_hbm, wu_ref, load_sem.at[5]),
    ]
    for load in loads:
        load.start()

    def rank_block(b, carry):
        owner = owner_ref[b]
        count = jnp.int32(0)
        for other in range(32):
            count += jnp.where((owner_ref[other] == owner) & (other < b), 1, 0)
        tgt[b] = jnp.minimum(owner * 2 + count, 63)
        return carry

    lax.fori_loop(0, 32, rank_block, 0)

    for load in loads:
        load.wait()
    for k in range(8):
        wd_s[:, pl.ds(k * 128, 128)] = wd_ref[k].astype(F32).T.astype(BF16)

    def place_pair(i, carry):
        for g in range(3):
            row = pl.ds(i * 3 + g, 1)
            place = (coff_ref[row, :] * 64 + pslot_ref[row, :]).astype(F32)
            column = jnp.broadcast_to(place, (128, 128)).T
            lanes = lax.broadcasted_iota(jnp.int32, (128, 128), 1).astype(F32)
            for k in range(4):
                chosen[pl.ds(i * 384 + g * 128, 128), pl.ds(k * 128, 128)] = jnp.where(
                    column == lanes + float(k * 128), 1.0, 0.0
                ).astype(BF16)
        turned = []
        for half in range(2):
            sites = pl.ds(i * 384 + half * 192, 192)
            both = jnp.concatenate([feats[sites, :], cotan[sites, :]], axis=1)
            turned.append(
                lax.dot_general(
                    both, chosen[sites, :], TN, preferred_element_type=F32
                ).astype(BF16)
            )
        parents = pl.ds(i * 128, 128)
        for k in range(8):
            rows, lanes = pl.ds(k * 128, 128), slice(k * 64, (k + 1) * 64)
            tile = jnp.concatenate([turned[0][:, lanes], turned[1][:, lanes]], axis=1)
            feat_t[rows, parents] = tile[0:128]
            cot_t[rows, parents] = tile[128:256]
        return carry

    lax.fori_loop(0, 16, place_pair, 0)

    wu_t = jnp.concatenate([wu_ref[k] for k in range(8)], axis=1)

    def up_tile(i, carry):
        rows = pl.ds(pl.multiple_of(i * 256, 256), 256)
        x_s[rows, :] = jnp.dot(wu_t, cot_t[:, rows], preferred_element_type=F32).T
        return carry

    lax.fori_loop(0, 8, up_tile, 0)

    def send_a(q, other):
        pltpu.make_async_remote_copy(
            src_ref=quarter.at[q, other], dst_ref=rec_a.at[q, m],
            send_sem=a_send.at[q], recv_sem=a_recv.at[q],
            device_id=(other // 2, chip * 2 + other % 2), device_id_type=MESH,
        ).start()

    def start_a(q):
        rec_a[q, m] = quarter[q, m]

    def bytes_of(ref, sem):
        return pltpu.make_async_copy(ref, ref, sem)

    def next_b(q):
        bytes_of(rec_a.at[q, pl.ds(0, 7)], a_recv.at[q]).wait()
        total = rec_a[q, 0].astype(F32)
        for other in range(1, 8):
            total += rec_a[q, other].astype(F32)
        bias = total[128:136] + total[136:144]
        for n in range(16):
            msg_b[q, n, 0:8] = total[n * 8 : (n + 1) * 8]
            msg_b[q, n, 8:16] = bias

        def step(d, carry):
            other, device = chip_peer(d)
            pltpu.make_async_remote_copy(
                src_ref=msg_b.at[q, other], dst_ref=rec_b.at[q, chip],
                send_sem=b_send.at[q], recv_sem=b_recv.at[q],
                device_id=device, device_id_type=MESH,
            ).start()
            return carry

        lax.fori_loop(1, 16, step, 0)
        rec_b[q, chip] = msg_b[q, chip]

    def next_c(q):
        bytes_of(rec_b.at[q, pl.ds(0, 15)], b_recv.at[q]).wait()
        total = rec_b[q, 0]
        for other in range(1, 16):
            total += rec_b[q, other]
        total = total * scale
        mine = pl.ds(pl.multiple_of(chip * 8, 8), 8)
        part[q, mine] = total[0:8]
        if q >= 2:
            bias_out[:, pl.ds((q % 2) * 128, 128)] = jnp.sum(total[8:16], axis=0, keepdims=True)

        def step(d, carry):
            _, device = chip_peer(d)
            pltpu.make_async_remote_copy(
                src_ref=part.at[q, mine], dst_ref=part.at[q, mine],
                send_sem=c_send.at[q], recv_sem=c_recv.at[q],
                device_id=device, device_id_type=MESH,
            ).start()
            return carry

        lax.fori_loop(1, 16, step, 0)

    def own_tile(q):
        return pltpu.make_async_copy(
            mine_s.at[q], tiles_out.at[q, m], store_sem.at[q]
        )

    def next_d(q):
        bytes_of(part.at[q, pl.ds(0, 120)], c_recv.at[q]).wait()
        block = part[q].T if q < 2 else part[q]
        mine_s[q] = block.astype(BF16)

        def step(d, carry):
            _, device = group_peer(d)
            pltpu.make_async_remote_copy(
                src_ref=mine_s.at[q], dst_ref=tiles_out.at[q, m],
                send_sem=d_send.at[q], recv_sem=d_recv.at[q],
                device_id=device, device_id_type=MESH,
            ).start()
            return carry

        lax.fori_loop(1, 8, step, 0)
        own_tile(q).start()

    def finish(q):
        own_tile(q).wait()
        seven = tiles_out.at[q, pl.ds(0, 7)]
        bytes_of(seven, d_recv.at[q]).wait()
        bytes_of(seven, d_send.at[q]).wait()
        bytes_of(rec_a.at[q, pl.ds(0, 7)], a_send.at[q]).wait()
        bytes_of(rec_b.at[q, pl.ds(0, 15)], b_send.at[q]).wait()
        bytes_of(part.at[q, pl.ds(0, 120)], c_send.at[q]).wait()
        bytes_of_round(q, x_send).wait()

    def products(q, left, right):
        def tile(i, carry):
            term = jnp.dot(left[pl.ds(i * 256, 256), :], right, preferred_element_type=F32)
            quarter[q, 2 * i, 0:128] = term[0:128].astype(BF16)
            quarter[q, 2 * i + 1, 0:128] = term[128:256].astype(BF16)
            for other in (2 * i, 2 * i + 1):
                @pl.when(other != m)
                def _():
                    send_a(q, other)
            return carry

        lax.fori_loop(0, 4, tile, 0)

    def up_round(q):
        half = pl.ds((q % 2) * 128, 128)
        wait_round(q)

        def pair(i, carry):
            rows = pl.ds(i * 128, 128)
            pre = jnp.concatenate(
                [recv[q][tgt[2 * i]], recv[q][tgt[2 * i + 1]]], axis=0
            ).astype(F32)
            sig = jax.nn.sigmoid(pre)
            slope_s[rows, half] = sig * (1.0 + pre * (1.0 - sig))
            act_s[rows, :] = (pre * sig).astype(BF16)
            return carry

        lax.fori_loop(0, 16, pair, 0)

        for other in range(8):
            quarter[q, other, 128:144] = jnp.zeros((16, 128), BF16)
        products(q, cot_t, act_s[...])

    def down_round(q):
        half = pl.ds((q % 2) * 128, 128)
        wait_round(q)

        def pair(i, bias):
            rows = pl.ds(i * 128, 128)
            deep = jnp.concatenate(
                [recv[q][tgt[2 * i]], recv[q][tgt[2 * i + 1]]], axis=0
            ).astype(F32)
            grad = ((deep + x_s[rows, half]) * slope_s[rows, half]).astype(BF16)
            pg_s[rows, half] = grad
            return bias + jnp.sum(grad.astype(F32).reshape(8, 16, 128), axis=0)

        bias = lax.fori_loop(0, 16, pair, jnp.zeros((16, 128), F32))

        for other in range(8):
            quarter[q, other, 128:144] = bias.astype(BF16)
        products(q, feat_t, pg_s[:, half])

    def fine_rows(first, last):
        def four(i, carry):
            grads = jnp.dot(
                pg_s[pl.ds(i * 256, 256), :], wd_s[...], preferred_element_type=F32
            ).astype(BF16)
            for j in range(4):
                stacked = jnp.concatenate(
                    [grads[j * 64 : (j + 1) * 64, k * 128 : (k + 1) * 128] for k in range(8)],
                    axis=0,
                )
                sites = pl.ds(i * 768 + j * 192, 192)
                fine_s[sites, :] = jnp.dot(
                    chosen[sites, :], stacked, preferred_element_type=F32
                ).astype(BF16)
            return carry

        lax.fori_loop(first, last, four, 0)

    def fine_copy():
        return pltpu.make_async_copy(fine_s, fine_out, store_sem.at[4])

    up_round(0)
    start_a(0)
    up_round(1)
    start_a(1)
    down_round(2)
    start_a(2)
    next_b(0)
    next_b(1)
    down_round(3)
    start_a(3)
    next_b(2)
    next_c(0)
    next_c(1)
    fine_rows(0, 3)
    next_b(3)
    next_d(0)
    next_d(1)
    next_c(2)
    next_c(3)
    next_d(2)
    next_d(3)
    fine_rows(3, 8)
    fine_copy().start()
    for q in range(4):
        finish(q)
    fine_copy().wait()


def on_device(
    fine_feats, out_grad, pre_act, deep_grad, down_weight, up_weight,
    block_owner, parent_slot, child_offset,
):
    devices = lax.axis_size("scene") * lax.axis_size("crop")
    sites = fine_feats.shape[1]
    scale = float(devices * sites) ** (-0.5)
    hbm = pl.BlockSpec(memory_space=pl.ANY)
    vmem = pl.BlockSpec(memory_space=pltpu.VMEM)
    dma = pltpu.SemaphoreType.DMA
    call = pl.pallas_call(
        functools.partial(level_kernel, scale),
        out_shape=(
            jax.ShapeDtypeStruct((sites, 128), BF16),
            jax.ShapeDtypeStruct((4, 8, 128, 128), BF16),
            jax.ShapeDtypeStruct((1, 256), F32),
        ),
        in_specs=[
            pl.BlockSpec(memory_space=pltpu.SMEM), hbm, hbm, hbm, hbm, hbm, hbm, hbm, hbm,
        ],
        out_specs=(hbm, hbm, vmem),
        scratch_shapes=[
            pltpu.SMEM((32,), jnp.int32),
            pltpu.VMEM((sites // 128, 128), jnp.int32),
            pltpu.VMEM((sites // 128, 128), jnp.int32),
            pltpu.VMEM((8, 128, 256), BF16),
            pltpu.VMEM((8, 256, 128), BF16),
            pltpu.VMEM((sites, 128), BF16),
            pltpu.VMEM((sites, 128), BF16),
            pltpu.VMEM((64, 64, 128), BF16),
            pltpu.VMEM((64, 64, 128), BF16),
            pltpu.VMEM((64, 64, 128), BF16),
            pltpu.VMEM((64, 64, 128), BF16),
            pltpu.VMEM((sites, 512), BF16),
            pltpu.VMEM((1024, 2048), BF16),
            pltpu.VMEM((1024, 2048), BF16),
            pltpu.VMEM((2048, 256), F32),
            pltpu.VMEM((2048, 256), F32),
            pltpu.VMEM((2048, 128), BF16),
            pltpu.VMEM((2048, 256), BF16),
            pltpu.VMEM((256, 1024), BF16),
            pltpu.VMEM((sites, 128), BF16),
            pltpu.VMEM((4, 8, 144, 128), BF16),
            pltpu.VMEM((4, 8, 144, 128), BF16),
            pltpu.VMEM((4, 16, 16, 128), F32),
            pltpu.VMEM((4, 16, 16, 128), F32),
            pltpu.VMEM((4, 128, 128), F32),
            pltpu.VMEM((4, 128, 128), BF16),
            dma((6,)), dma((4,)), dma((4,)), dma((4,)),
            dma((4,)), dma((4,)), dma((4,)), dma((4,)),
            dma((4,)), dma((4,)), dma((4,)), dma((4,)), dma((5,)),
        ],
        compiler_params=pltpu.CompilerParams(
            collective_id=0, has_side_effects=True, vmem_limit_bytes=60 << 20
        ),
        cost_estimate=pl.CostEstimate(
            flops=12 * 10**9, bytes_accessed=16 * 10**6, transcendentals=10**6
        ),
    )
    fine, tiles, bias = call(
        block_owner.reshape(32),
        parent_slot.reshape(sites // 128, 128),
        child_offset.reshape(sites // 128, 128),
        fine_feats[0],
        out_grad[0],
        pre_act.reshape(64, 64, 256),
        deep_grad.reshape(64, 64, 256),
        down_weight,
        up_weight,
    )
    up = jnp.concatenate([tiles[0], tiles[1]], axis=1).astype(F32)
    down = jnp.concatenate([tiles[2], tiles[3]], axis=2).astype(F32)
    return fine[None], down, up, bias[0]


def solution(mesh):
    return jax.shard_map(
        on_device,
        mesh=mesh,
        in_specs=(
            P("crop", "scene", None),
            P("crop", "scene", None),
            P("crop", "scene", None, None, None, None),
            P("crop", "scene", None, None, None, None),
            P(),
            P(),
            P("crop", "scene", None),
            P("crop", "scene"),
            P("crop", "scene"),
        ),
        out_specs=(P("crop", "scene", None), P(), P(), P()),
        check_vma=False,
    )
```
